32 devices in a mesh: grp: 2 (over y), voc: 8 (over z, x), tok: 2 (over core).
Axes of the slice: x: 2, y: 2, z: 4, core: 2. Of those that a mesh axis runs over, the one named last changes fastest.
Arguments:
- target_hidden: bfloat16 [3072, 4096], P(('grp', 'tok'), 'voc'), parts along dimension 0, may hold values from -16 to 16
- draft_hidden: bfloat16 [3072, 896], P(('grp', 'tok'), 'voc'), parts along dimension 0, may hold values from -16 to 16
- target_head: bfloat16 [4096, 10240], P(None, 'voc'), may hold values from -1 to 1
- draft_head: bfloat16 [896, 10240], P('tok', 'voc'), may hold values from -1 to 1
Outputs:
- row_loss: float32 [3072], P(('grp', 'tok')), parts along dimension 0
- draft_grad: bfloat16 [1792, 10240], P(('grp', 'tok'), 'voc'), parts along dimension 0
The draws below stay inside these ranges and needn't reach their ends.
There are 2 independent parts, one for each index of `grp`. The reference program is written for one: setup_inputs(seed, part) draws one part's arguments, and reference() takes and returns one part's arrays. A program takes and returns all parts, laid end to end along the dimension named above; an argument that names none is the same for every part. Nothing has to cross between parts.
All inputs are finite; a program needn't handle non-finite values.
Results may differ from the reference program's by a relative error of at most 0.0085.
Values may be sent and summed in bfloat16 or wider, within the bound.
No kernel may reach another device: no remote copies, remote signals or barrier semaphores. Data moves between devices by JAX's collectives and lax.ppermute only.
A program may use at most 128 MiB of HBM per device.

```python
from functools import partial
import jax
import jax.numpy as jnp
from jax import lax

D = 4096
DD = 896
ROWS = 768
VOCAB = 10240
TOKENS = 1536
N_TOK = 2


def draw_target_hidden(key, part):
    key = jax.random.fold_in(key, 5)
    values = jnp.clip(3.0 * jax.random.normal(key, (TOKENS, D), jnp.float32), -16.0, 16.0)
    return values.astype(jnp.bfloat16)


def draw_draft_hidden(key, part):
    key = jax.random.fold_in(key, 6)
    values = jnp.clip(3.0 * jax.random.normal(key, (TOKENS, DD), jnp.float32), -16.0, 16.0)
    return values.astype(jnp.bfloat16)


def draw_target_head(key, part):
    key = jax.random.fold_in(key, 7)
    values = jax.random.normal(key, (D, VOCAB), jnp.float32) / jnp.sqrt(float(D))
    return jnp.clip(values, -1.0, 1.0).astype(jnp.bfloat16)


def draw_draft_head(key, part):
    key = jax.random.fold_in(key, 8)
    values = jax.random.normal(key, (DD, VOCAB), jnp.float32) / jnp.sqrt(float(DD))
    return jnp.clip(values, -1.0, 1.0).astype(jnp.bfloat16)


def setup_inputs(seed: int = 0, part: int = 0) -> dict:
    seeds = jax.random.split(jax.random.key(seed), 5)
    part_keys = jax.random.split(jax.random.fold_in(seeds[4], part), 5)
    return {
        "target_hidden": draw_target_hidden(jax.random.fold_in(jax.random.fold_in(seeds[4], part), 71), part),
        "draft_hidden": draw_draft_hidden(jax.random.fold_in(jax.random.fold_in(seeds[4], part), 71), part),
        "target_head": draw_target_head(jax.random.fold_in(seeds[4], 71), part),
        "draft_head": draw_draft_head(jax.random.fold_in(seeds[4], 71), part),
    }


def block_terms(args, target_head, draft_head):
    hid_target, hid_draft = args
    full = float(VOCAB)
    target_logits = jnp.dot(hid_target, target_head, preferred_element_type=jnp.float32)
    draft_logits = jnp.dot(hid_draft, draft_head, preferred_element_type=jnp.float32)
    target_exp = jnp.exp(target_logits - lax.optimization_barrier(jnp.max(target_logits, axis=1, keepdims=True)))
    target_prob = target_exp / lax.optimization_barrier(jnp.sum(target_exp, axis=1, keepdims=True))
    draft_exp = jnp.exp(draft_logits - lax.optimization_barrier(jnp.max(draft_logits, axis=1, keepdims=True)))
    draft_prob = draft_exp / lax.optimization_barrier(jnp.sum(draft_exp, axis=1, keepdims=True))
    spread = full * (draft_prob - target_prob)
    root = jnp.sqrt(spread * spread + 1.0)
    slope = spread / root
    loss = lax.optimization_barrier(jnp.sum(root - 1.0, axis=1)) / (2.0 * full)
    inner = lax.optimization_barrier(jnp.sum(draft_prob * slope, axis=1, keepdims=True))
    logit_grad = (full * draft_prob * (slope - inner)).astype(jnp.bfloat16)
    return (loss, logit_grad)

def reference(target_hidden, draft_hidden, target_head, draft_head):
    hid_target = target_hidden.reshape(N_TOK, ROWS, D)
    hid_draft = draft_hidden.reshape(N_TOK, ROWS, DD)
    loss, logit_grad = lax.map(partial(block_terms, target_head=target_head, draft_head=draft_head), (hid_target, hid_draft))
    row_loss = loss.reshape(TOKENS)
    logit_grad = logit_grad.reshape(TOKENS, VOCAB)
    summed = lax.dot_general(draft_hidden, logit_grad, (((0,), (0,)), ((), ())), preferred_element_type=jnp.float32)
    draft_grad = (summed / float(TOKENS)).astype(jnp.bfloat16)
    return (row_loss, draft_grad)
```

```python
import functools

import jax
import jax.numpy as jnp
from jax import lax
from jax.experimental import pallas as pl
from jax.experimental.pallas import tpu as pltpu
from jax.sharding import PartitionSpec as P

F32, BF16 = jnp.float32, jnp.bfloat16
VMEM_BYTES = 48 * 2**20
LANES = 128


def _eye(n):
    return lax.broadcasted_iota(jnp.int32, (n, n), 0) == lax.broadcasted_iota(jnp.int32, (n, n), 1)


def _to_row(eye, column):
    return jnp.sum(jnp.where(eye, column, 0.0), axis=0, keepdims=True)


def _to_column(eye, row):
    return jnp.sum(jnp.where(eye, row, 0.0), axis=1, keepdims=True)


def _dot(a, b):
    return jnp.dot(a, b, preferred_element_type=F32)


def _products(xs, wts, wds, feats):
    target = _dot(xs[0][:, :feats], wts[0][...])
    for x, w in zip(xs[1:], wts[1:], strict=True):
        target += _dot(x[:, :feats], w[...])
    draft = _dot(
        jnp.concatenate([x[:, feats:] for x in xs], axis=1),
        jnp.concatenate([w[...] for w in wds], axis=0),
    )
    return target, draft


def _near_kernel(feats, perm, x0, x1, x2, x3, w0, w1, w2, w3, d0, d1, d2, d3, acc_t, acc_d):
    target, draft = _products((x0, x1, x2, x3), (w0, w1, w2, w3), (d0, d1, d2, d3), feats)
    acc_t[...] = target
    acc_d[...] = draft


def _near(perm, own, p1, o, a, wt, wd, half, tile, feats):
    half_rows, width = p1.shape
    vocab = wt.shape[1]
    steps = half_rows // tile
    piece = lambda off: pl.BlockSpec((tile, width), lambda i, p: (i + off, 0))
    w_spec = lambda k: pl.BlockSpec((feats, vocab), lambda i, p: (p[k], 0))
    d_spec = lambda k: pl.BlockSpec((width - feats, vocab), lambda i, p: (p[k], 0))
    out = pl.BlockSpec((tile, vocab), lambda i, p: (i, 0))
    return pl.pallas_call(
        functools.partial(_near_kernel, feats),
        grid_spec=pltpu.PrefetchScalarGridSpec(
            num_scalar_prefetch=1,
            grid=(steps,),
            in_specs=[piece(half * steps), piece(0), piece(0), piece(0)]
            + [w_spec(k) for k in range(4)]
            + [d_spec(k) for k in range(4)],
            out_specs=[out, out],
        ),
        out_shape=[jax.ShapeDtypeStruct((half_rows, vocab), F32)] * 2,
        compiler_params=pltpu.CompilerParams(vmem_limit_bytes=VMEM_BYTES),
        cost_estimate=pl.CostEstimate(
            flops=2 * half_rows * 4 * width * vocab,
            bytes_accessed=8 * width * vocab + 8 * half_rows * vocab + 8 * half_rows * width,
            transcendentals=0,
        ),
        name="near_logits",
    )(perm, own, p1, o, a, *[wt] * 4, *[wd] * 4)


def _far_kernel(feats, chunk, first, perm, *refs):
    xs, wts, wds, (in_t, in_d) = refs[0:4], refs[4:8], refs[8:12], refs[12:14]
    refs = refs[14 if first else 16 :]
    stats_in = None if first else refs[0]
    e_t, e_d, stats = refs[0 if first else 1 :]
    j, steps = pl.program_id(0), pl.num_programs(0)
    rows, cols = in_t.shape
    target, draft = _products(xs, wts, wds, feats)
    here = pl.ds(pl.multiple_of(j * cols, cols), cols)
    e_t[:, here] = target + in_t[...]
    e_d[:, here] = draft + in_d[...]

    @pl.when(j == steps - 1)
    def _():
        eye = _eye(rows)
        if first:
            stats[...] = jnp.zeros_like(stats)
        else:
            stats[...] = stats_in[...]
        for kind, ref in enumerate((e_t, e_d)):
            logits = ref[...]
            top = jnp.max(logits, axis=1, keepdims=True)
            e = jnp.exp(logits - top)
            ref[...] = e
            row = 2 * chunk + kind
            stats[0, row : row + 1, :] = _to_row(eye, top)
            stats[1, row : row + 1, :] = _to_row(eye, jnp.sum(e, axis=1, keepdims=True))


def _far(perm, far, f, wt, wd, acc, prev, chunk, chunks, feats, cols):
    rows2, width = far.shape
    rows, vocab = rows2 // 2, wt.shape[1]
    first = prev is None
    piece = lambda half: pl.BlockSpec((rows, width), lambda j, p: (half, 0))
    w_spec = lambda k: pl.BlockSpec((feats, cols), lambda j, p: (p[k], j))
    d_spec = lambda k: pl.BlockSpec((width - feats, cols), lambda j, p: (p[k], j))
    in_half = chunk % (acc[0].shape[0] // rows)
    acc_spec = pl.BlockSpec((rows, cols), lambda j, p: (in_half, j))
    e_spec = pl.BlockSpec((rows, vocab), lambda j, p: (chunk, 0))
    s_spec = pl.BlockSpec((2, 2 * chunks, rows), lambda j, p: (0, 0, 0))
    anywhere = pl.BlockSpec(memory_space=pl.ANY)
    return pl.pallas_call(
        functools.partial(_far_kernel, feats, chunk, first),
        grid_spec=pltpu.PrefetchScalarGridSpec(
            num_scalar_prefetch=1,
            grid=(vocab // cols,),
            in_specs=[piece(0), piece(1), piece(0), piece(1)]
            + [w_spec(k) for k in range(4, 8)]
            + [d_spec(k) for k in range(4, 8)]
            + [acc_spec, acc_spec]
            + ([] if first else [anywhere, anywhere, s_spec]),
            out_specs=[e_spec, e_spec, s_spec],
        ),
        out_shape=[jax.ShapeDtypeStruct((chunks * rows, vocab), F32)] * 2
        + [jax.ShapeDtypeStruct((2, 2 * chunks, rows), F32)],
        input_output_aliases={} if first else {15: 0, 16: 1},
        compiler_params=pltpu.CompilerParams(vmem_limit_bytes=VMEM_BYTES),
        cost_estimate=pl.CostEstimate(
            flops=2 * rows * 4 * width * vocab,
            bytes_accessed=8 * width * vocab + 16 * rows * vocab + 8 * rows * width,
            transcendentals=2 * rows * vocab,
        ),
        name="far_logits",
    )(perm, far, far, f, f, *[wt] * 4, *[wd] * 4, *acc, *(() if first else prev))


def _slope_kernel(full, e_t, e_d, mine, total, slope_out, scaled_out, sums):
    i = pl.program_id(0)
    rows = e_t.shape[0]
    eye = _eye(rows)

    def scale(kind):
        row = pl.ds(2 * i + kind, 1)
        return _to_column(eye, jnp.exp(mine[0, row, :] - total[0, row, :]) / total[1, row, :])

    target = e_t[...] * (scale(0) * full)
    draft = e_d[...] * (scale(1) * full)
    spread = draft - target
    square = spread * spread + 1.0
    inverse = lax.rsqrt(square)
    slope = spread * inverse
    slope_out[...] = slope
    scaled_out[...] = draft
    loss = jnp.sum(square * inverse - 1.0, axis=1, keepdims=True) * (1.0 / (2.0 * full))
    inner = jnp.sum(draft * slope, axis=1, keepdims=True) * (1.0 / full)
    sums[pl.ds(2 * i, 1), :] = _to_row(eye, loss)
    sums[pl.ds(2 * i + 1, 1), :] = _to_row(eye, inner)


def _slopes(e_t, e_d, mine, total, chunks, full):
    rows_all, vocab = e_t.shape
    rows = rows_all // chunks
    block = pl.BlockSpec((rows, vocab), lambda i: (i, 0))
    whole = pl.BlockSpec(mine.shape, lambda i: (0, 0, 0))
    return pl.pallas_call(
        functools.partial(_slope_kernel, full),
        grid=(chunks,),
        in_specs=[block, block, whole, whole],
        out_specs=[block, block, pl.BlockSpec((2 * chunks, rows), lambda i: (0, 0))],
        out_shape=[jax.ShapeDtypeStruct((rows_all, vocab), F32)] * 2
        + [jax.ShapeDtypeStruct((2 * chunks, rows), F32)],
        input_output_aliases={0: 0, 1: 1},
        compiler_params=pltpu.CompilerParams(vmem_limit_bytes=VMEM_BYTES),
        cost_estimate=pl.CostEstimate(
            flops=12 * rows_all * vocab, bytes_accessed=16 * rows_all * vocab, transcendentals=rows_all * vocab
        ),
        name="slopes",
    )(e_t, e_d, mine, total)


def _turn_kernel(chunks, perm, own, p1a, p1b, oa, ob, aa, ab, *refs):
    fars, fs, out = refs[:chunks], refs[chunks : 2 * chunks], refs[2 * chunks]
    half = p1a.shape[0]
    rows = fars[0].shape[0] // 2

    def put(k, start, value):
        place = pl.ds(pl.multiple_of(perm[k] * LANES, LANES), LANES)
        out[place, start : start + value.shape[0]] = jnp.transpose(value)

    put(0, 0, own[...])
    for k, pair in enumerate(((p1a, p1b), (oa, ob), (aa, ab))):
        put(k + 1, 0, pair[0][...])
        put(k + 1, half, pair[1][...])
    for k, parts in ((4, fars), (6, fs)):
        for c in range(chunks):
            put(k, c * rows, parts[c][:rows, :])
            put(k + 1, c * rows, parts[c][rows:, :])


def _turn(perm, own, halves, fars, fs, feats):
    rows_all = own.shape[0]
    column = feats // LANES
    spec = lambda x: pl.BlockSpec((x.shape[0], LANES), lambda i, p: (0, column))
    arrays = [own, *halves, *fars, *fs]
    return pl.pallas_call(
        functools.partial(_turn_kernel, len(fars)),
        grid_spec=pltpu.PrefetchScalarGridSpec(
            num_scalar_prefetch=1,
            grid=(1,),
            in_specs=[spec(x) for x in arrays],
            out_specs=pl.BlockSpec((8 * LANES, rows_all), lambda i, p: (0, 0)),
        ),
        out_shape=jax.ShapeDtypeStruct((8 * LANES, rows_all), BF16),
        compiler_params=pltpu.CompilerParams(vmem_limit_bytes=VMEM_BYTES),
        cost_estimate=pl.CostEstimate(
            flops=16 * LANES * rows_all, bytes_accessed=32 * LANES * rows_all, transcendentals=0
        ),
        name="turned_features",
    )(perm, *arrays)


def _send_kernel(chunks, tokens, tok, features, slope, scaled, inner, grad_out, part_out, column):
    rows = inner.shape[1]

    @pl.when(pl.program_id(0) == 0)
    def _():
        eye = _eye(rows)
        for c in range(chunks):
            column[c * rows : (c + 1) * rows, :] = _to_column(eye, inner[2 * c + 1 : 2 * c + 2, :])

    grad = (scaled[...] * (slope[...] - column[...])).astype(BF16)
    grad_out[...] = grad
    part_out[...] = (_dot(features[...], grad) * (1.0 / tokens)).astype(part_out.dtype)


def _send(tok, features, slope, scaled, inner, chunks, tokens, cols):
    rows_all, vocab = slope.shape
    half = features.shape[0] // 2
    block = pl.BlockSpec((rows_all, cols), lambda j, t: (0, j))
    return pl.pallas_call(
        functools.partial(_send_kernel, chunks, tokens),
        grid_spec=pltpu.PrefetchScalarGridSpec(
            num_scalar_prefetch=1,
            grid=(vocab // cols,),
            in_specs=[
                pl.BlockSpec((half, rows_all), lambda j, t: (1 - t[0], 0)),
                block,
                block,
                pl.BlockSpec(inner.shape, lambda j, t: (0, 0)),
            ],
            out_specs=[block, pl.BlockSpec((half, cols), lambda j, t: (0, j))],
            scratch_shapes=[pltpu.VMEM((rows_all, 1), F32)],
        ),
        out_shape=[
            jax.ShapeDtypeStruct((rows_all, vocab), BF16),
            jax.ShapeDtypeStruct((half, vocab), BF16),
        ],
        compiler_params=pltpu.CompilerParams(vmem_limit_bytes=VMEM_BYTES),
        cost_estimate=pl.CostEstimate(
            flops=2 * half * rows_all * vocab,
            bytes_accessed=10 * rows_all * vocab + 2 * half * (vocab + rows_all),
            transcendentals=0,
        ),
        name="gradient_to_send",
    )(tok, features, slope, scaled, inner)


def _keep_kernel(tokens, tok, features, grad, out):
    out[...] = _dot(features[...], grad[...]) * (1.0 / tokens)


def _keep(tok, features, grad, tokens, cols):
    rows_all, vocab = grad.shape
    half = features.shape[0] // 2
    return pl.pallas_call(
        functools.partial(_keep_kernel, tokens),
        grid_spec=pltpu.PrefetchScalarGridSpec(
            num_scalar_prefetch=1,
            grid=(vocab // cols,),
            in_specs=[
                pl.BlockSpec((half, rows_all), lambda j, t: (t[0], 0)),
                pl.BlockSpec((rows_all, cols), lambda j, t: (0, j)),
            ],
            out_specs=pl.BlockSpec((half, cols), lambda j, t: (0, j)),
        ),
        out_shape=jax.ShapeDtypeStruct((half, vocab), F32),
        compiler_params=pltpu.CompilerParams(vmem_limit_bytes=VMEM_BYTES),
        cost_estimate=pl.CostEstimate(
            flops=2 * half * rows_all * vocab,
            bytes_accessed=2 * rows_all * vocab + 2 * half * rows_all + 4 * half * vocab,
            transcendentals=0,
        ),
        name="gradient_to_keep",
    )(tok, features, grad)


class _Slots:
    def __init__(self):
        self.before, self.last, self.now = [], [], []

    def next(self):
        self.before, self.last, self.now = self.last, self.now, []

    def move(self, x, pairs):
        if self.before:
            x = lax.optimization_barrier((x, *self.before))[0]
        y = lax.ppermute(x, "voc", pairs)
        self.now.append(y)
        return y


def _xor(k):
    return [(i, i ^ k) for i in range(8)]


MIDDLE = [(2, 4), (4, 2), (3, 5), (5, 3)]
OUTWARD = [(2, 0), (3, 1), (4, 6), (5, 7)]


def _gather(own, z):
    rows = own.shape[0] // 4
    end = (z == 0) | (z == 3)
    slots = _Slots()
    halves = [own[: 2 * rows], own[2 * rows :]]
    p1, o, a, middle, outward, far, f = [], [], [], [], [], [], []

    def near(c):
        start = (c % 2) * rows
        return jnp.concatenate([h[start : start + rows] for h in (halves[c // 2], p1[c // 2])])

    for slot in range(8):
        if slot < 2:
            p1.append(slots.move(halves[slot], _xor(2)))
            o.append(slots.move(halves[slot], _xor(1)))
        elif slot < 4:
            a.append(slots.move(p1[slot - 2], _xor(1)))
        if 2 <= slot < 6:
            outward.append(slots.move(middle[slot - 2], OUTWARD))
        if 1 <= slot < 5:
            middle.append(slots.move(near(slot - 1), MIDDLE))
        if slot >= 4:
            c = slot - 4
            far.append(jnp.where(end, outward[c], middle[c]))
            f.append(slots.move(far[c], _xor(1)))
        slots.next()
    return p1, o, a, far, f


def _all_reduce(x, merge):
    for k in (1, 2, 4):
        x = merge(x, lax.ppermute(x, "voc", _xor(k)))
    return x


def _merge_softmax(a, b):
    top = jnp.maximum(a[0], b[0])
    return jnp.stack([top, a[1] * jnp.exp(a[0] - top) + b[1] * jnp.exp(b[0] - top)])


def _body_4x2(target_hidden, draft_hidden, target_head, draft_head):
    rows_all, feats = target_hidden.shape
    draft_feats = draft_hidden.shape[1]
    vocab = target_head.shape[1]
    chunks, cols = 4, 256
    rows = rows_all // chunks
    full = float(vocab * lax.axis_size("voc"))
    tokens = float(rows_all * lax.axis_size("tok"))
    me, tok = lax.axis_index("voc"), lax.axis_index("tok")
    z, x = me // 2, me % 2

    far_z = jnp.where(z < 2, jnp.array([2, 3]), jnp.array([1, 0]))
    perm = jnp.stack(
        [me, me ^ 2, me ^ 1, me ^ 3]
        + [far_z[0] * 2 + x, far_z[1] * 2 + x, far_z[0] * 2 + 1 - x, far_z[1] * 2 + 1 - x]
    ).astype(jnp.int32)
    tok_index = tok.reshape(1).astype(jnp.int32)

    own = jnp.concatenate(
        [target_hidden, jnp.pad(draft_hidden, ((0, 0), (0, LANES - draft_feats)))], axis=1
    )
    p1, o, a, far, f = _gather(own, z)

    other_head = lax.ppermute(draft_head, "tok", [(0, 1), (1, 0)])
    head = jnp.where(tok == 0, jnp.stack([draft_head, other_head]), jnp.stack([other_head, draft_head]))
    head = jnp.pad(head.reshape(8, draft_feats, vocab), ((0, 0), (0, LANES - draft_feats), (0, 0)))
    head = head.reshape(8 * LANES, vocab)

    acc = [_near(perm, own, p1[h], o[h], a[h], target_head, head, h, rows, feats) for h in range(2)]
    state = None
    for c in range(chunks):
        state = _far(perm, far[c], f[c], target_head, head, acc[c // 2], state, c, chunks, feats, cols)
    e_t, e_d, mine = state
    total = _all_reduce(mine, _merge_softmax)
    slope, scaled, sums = _slopes(e_t, e_d, mine, total, chunks, full)
    features = _turn(perm, own, [*p1, *o, *a], far, f, feats)
    sums = _all_reduce(sums, jnp.add)
    row_loss = sums.reshape(chunks, 2, rows)[:, 0].reshape(rows_all)
    grad, send = _send(tok_index, features, slope, scaled, sums, chunks, tokens, cols)
    received = lax.ppermute(send, "tok", [(0, 1), (1, 0)])
    keep = _keep(tok_index, features, grad, tokens, cols)
    draft_grad = (keep + received.astype(F32)).astype(BF16)
    draft_grad = draft_grad.reshape(4, LANES, vocab)[:, :draft_feats].reshape(4 * draft_feats, vocab)
    return row_loss, draft_grad


def _body_any(target_hidden, draft_hidden, target_head, draft_head):
    rows, vocab = target_hidden.shape[0], target_head.shape[1]
    full = float(vocab * lax.axis_size("voc"))
    tokens = float(rows * lax.axis_size("tok"))
    draft_weights = lax.all_gather(draft_head, "tok", axis=0, tiled=True)
    hidden = lax.all_gather(target_hidden, "voc", axis=1, tiled=True)
    target_logits = jnp.dot(hidden, target_head, preferred_element_type=F32)
    features = lax.all_gather(draft_hidden, "voc", axis=1, tiled=True)
    draft_logits = jnp.dot(features, draft_weights, preferred_element_type=F32)
    top_t, top_d = lax.pmax((jnp.max(target_logits, axis=1), jnp.max(draft_logits, axis=1)), "voc")
    target_exp = jnp.exp(target_logits - top_t[:, None])
    draft_exp = jnp.exp(draft_logits - top_d[:, None])
    total_t, total_d = lax.psum((jnp.sum(target_exp, axis=1), jnp.sum(draft_exp, axis=1)), "voc")
    target_prob = target_exp / total_t[:, None]
    draft_prob = draft_exp / total_d[:, None]
    spread = full * (draft_prob - target_prob)
    root = jnp.sqrt(spread * spread + 1.0)
    slope = spread / root
    loss = jnp.sum(root - 1.0, axis=1) / (2.0 * full)
    row_loss, inner = lax.psum((loss, jnp.sum(draft_prob * slope, axis=1)), "voc")
    logit_grad = (full * draft_prob * (slope - inner[:, None])).astype(BF16)
    summed = lax.dot_general(features, logit_grad, (((0,), (0,)), ((), ())), preferred_element_type=F32)
    draft_grad = lax.psum_scatter((summed / tokens).astype(BF16), "tok", scatter_dimension=0, tiled=True)
    return row_loss, draft_grad


def solution(mesh):
    body = _body_4x2 if (mesh.shape["voc"], mesh.shape["tok"]) == (8, 2) else _body_any
    return jax.shard_map(
        body,
        mesh=mesh,
        in_specs=(
            P(("grp", "tok"), "voc"),
            P(("grp", "tok"), "voc"),
            P(None, "voc"),
            P("tok", "voc"),
        ),
        out_specs=(P(("grp", "tok")), P(("grp", "tok"), "voc")),
        check_vma=False,
    )
```

```python
import functools

import jax
import jax.numpy as jnp
from jax import lax
from jax.experimental import pallas as pl
from jax.experimental.pallas import tpu as pltpu
from jax.sharding import PartitionSpec as P

F32, BF16 = jnp.float32, jnp.bfloat16
SCOPED_BYTES = 12 * 2**20
LANES = 128
BLOCK = 32

VMEM = pl.BlockSpec(memory_space=pltpu.VMEM)
SMEM = pl.BlockSpec(memory_space=pltpu.SMEM)
ANYWHERE = pl.BlockSpec(memory_space=pl.ANY)


def _kernel(body, outs, ins, name, flops=0, scratch=(), specs=None, out_specs=None, exps=0):
    specs = specs or [VMEM] * len(ins)
    ins = [pltpu.with_memory_space_constraint(x, pltpu.VMEM) if s is VMEM else x for x, s in zip(ins, specs, strict=True)]
    return pl.pallas_call(
        body,
        in_specs=specs,
        out_specs=out_specs or [VMEM] * len(outs),
        out_shape=outs,
        scratch_shapes=scratch,
        compiler_params=pltpu.CompilerParams(vmem_limit_bytes=SCOPED_BYTES),
        cost_estimate=pl.CostEstimate(
            flops=flops,
            bytes_accessed=sum(x.size * x.dtype.itemsize for x in ins),
            transcendentals=exps,
        ),
        name=name,
    )(*ins)


def _eye(n):
    return lax.broadcasted_iota(jnp.int32, (n, n), 0) == lax.broadcasted_iota(jnp.int32, (n, n), 1)


def _to_row(eye, column):
    return jnp.sum(jnp.where(eye, column, 0.0), axis=0, keepdims=True)


def _to_column(eye, row):
    return jnp.sum(jnp.where(eye, row, 0.0), axis=1, keepdims=True)


def _dot(a, b):
    return jnp.dot(a, b, preferred_element_type=F32)


def _place(index, size):
    return pl.ds(pl.multiple_of(index * size, size), size)


def _pack_kernel(target, draft, low, high):
    half, feats, draft_feats = low.shape[0], target.shape[1], draft.shape[1]
    for start, out in ((0, low), (half, high)):
        out[:, :feats] = target[start : start + half, :]
        out[:, feats:] = jnp.zeros((half, LANES), BF16)
        out[:, feats : feats + draft_feats] = draft[start : start + half, :]


def _pack(target, draft):
    rows, feats = target.shape
    out = pltpu.VMEM((rows // 2, feats + LANES), BF16)
    plain = pl.BlockSpec()
    return _kernel(_pack_kernel, [out, out], [target, draft], "packed_hidden", specs=[plain, plain])


def _fetch_kernel(source, out, sem):
    copy = pltpu.make_async_copy(source, out, sem)
    copy.start()
    copy.wait()


def _fetch(x):
    return _kernel(
        _fetch_kernel, [pltpu.VMEM(x.shape, x.dtype)], [x], "target_head", specs=[ANYWHERE], scratch=[pltpu.SemaphoreType.DMA]
    )[0]


def _head_kernel(tok, mine, other, out):
    part = mine.shape[0] // 4
    out[...] = jnp.zeros_like(out)
    for which, ref in ((tok[0], mine), (1 - tok[0], other)):
        for b in range(4):
            start = pl.multiple_of(which * (4 * LANES) + b * LANES, LANES)
            out[pl.ds(start, part), :] = ref[b * part : (b + 1) * part, :]


def _head(tok, mine, other):
    plain = pl.BlockSpec()
    return _kernel(
        _head_kernel,
        [pltpu.VMEM((8 * LANES, mine.shape[1]), BF16)],
        [tok, mine, other],
        "draft_head",
        specs=[SMEM, plain, VMEM],
    )[0]


def _products(perm, xs, first, wt, wd, cols):
    feats = xs[0].shape[1] - LANES
    target = None
    for k, x in enumerate(xs):
        term = _dot(x[:, :feats], wt[_place(perm[first + k], feats), cols])
        target = term if target is None else target + term
    draft = _dot(
        jnp.concatenate([x[:, feats:] for x in xs], axis=1),
        jnp.concatenate([wd[_place(perm[first + k], LANES), cols] for k in range(len(xs))], axis=0),
    )
    return target, draft


def _columns(vocab, cols):
    return [slice(n, n + cols) for n in range(0, vocab, cols)]


def _near_kernel(perm, x0, x1, x2, x3, wt, wd, acc_t, acc_d):
    for c in _columns(wt.shape[1], 256):
        acc_t[:, c], acc_d[:, c] = _products(perm, (x0, x1, x2, x3), 0, wt, wd, c)


def _near(perm, own, p1, o, a, wt, wd):
    rows, vocab = own.shape[0], wt.shape[1]
    out = pltpu.VMEM((rows, vocab), F32)
    return _kernel(
        _near_kernel,
        [out, out],
        [perm, own, p1, o, a, wt, wd],
        "near_logits",
        flops=8 * rows * own.shape[1] * vocab,
        specs=[SMEM] + [VMEM] * 6,
    )


def _far_kernel(chunk, perm, far, f, wt, wd, acc_t, acc_d, before, e_t, e_d, stats):
    rows = e_t.shape[0]
    at = (chunk % 2) * rows
    pieces = [ref.at[half * rows : (half + 1) * rows, :] for ref in (far, f) for half in (0, 1)]
    for c in _columns(wt.shape[1], 256):
        target, draft = _products(perm, pieces, 4, wt, wd, c)
        e_t[:, c] = target + acc_t[at : at + rows, c]
        e_d[:, c] = draft + acc_d[at : at + rows, c]
    eye = _eye(rows)
    stats[...] = before[...]
    for kind, ref in enumerate((e_t, e_d)):
        tops, sums = [], []
        for r in range(0, rows, BLOCK):
            logits = ref[r : r + BLOCK, :]
            top = jnp.max(logits, axis=1, keepdims=True)
            e = jnp.exp(logits - top)
            ref[r : r + BLOCK, :] = e
            tops.append(top)
            sums.append(jnp.sum(e, axis=1, keepdims=True))
        row = 2 * chunk + kind
        stats[0, row : row + 1, :] = _to_row(eye, jnp.concatenate(tops, axis=0))
        stats[1, row : row + 1, :] = _to_row(eye, jnp.concatenate(sums, axis=0))


def _far(chunk, perm, far, f, wt, wd, acc, before):
    rows, vocab = far.shape[0] // 2, wt.shape[1]
    out = pltpu.VMEM((rows, vocab), F32)
    return _kernel(
        functools.partial(_far_kernel, chunk),
        [out, out, pltpu.VMEM(before.shape, F32)],
        [perm, far, f, wt, wd, *acc, before],
        "far_logits",
        flops=8 * rows * far.shape[1] * vocab,
        exps=2 * rows * vocab,
        specs=[SMEM] + [VMEM] * 7,
    )


def _slope_kernel(full, *refs):
    chunks = (len(refs) - 5) // 2
    es_t, es_d = refs[:chunks], refs[chunks : 2 * chunks]
    mine, total, slope_out, scaled_out, sums = refs[2 * chunks :]
    rows = mine.shape[2]
    eye = _eye(rows)
    for i in range(chunks):
        scales = [
            full
            * _to_column(eye, jnp.exp(mine[0, r : r + 1, :] - total[0, r : r + 1, :]) / total[1, r : r + 1, :])
            for r in (2 * i, 2 * i + 1)
        ]
        losses, inners = [], []
        for r in range(0, rows, BLOCK):
            target = es_t[i][r : r + BLOCK, :] * scales[0][r : r + BLOCK]
            draft = es_d[i][r : r + BLOCK, :] * scales[1][r : r + BLOCK]
            spread = draft - target
            square = spread * spread + 1.0
            inverse = lax.rsqrt(square)
            slope = spread * inverse
            slope_out[i * rows + r : i * rows + r + BLOCK, :] = slope
            scaled_out[i * rows + r : i * rows + r + BLOCK, :] = draft
            losses.append(jnp.sum(square * inverse - 1.0, axis=1, keepdims=True))
            inners.append(jnp.sum(draft * slope, axis=1, keepdims=True))
        sums[2 * i : 2 * i + 1, :] = _to_row(eye, jnp.concatenate(losses, axis=0)) * (0.5 / full)
        sums[2 * i + 1 : 2 * i + 2, :] = _to_row(eye, jnp.concatenate(inners, axis=0)) * (1.0 / full)


def _slopes(es_t, es_d, mine, total, full):
    chunks, (rows, vocab) = len(es_t), es_t[0].shape
    out = pltpu.VMEM((chunks * rows, vocab), F32)
    return _kernel(
        functools.partial(_slope_kernel, full),
        [out, out, pltpu.VMEM((2 * chunks, rows), F32)],
        [*es_t, *es_d, mine, total],
        "slopes",
        flops=12 * chunks * rows * vocab,
        exps=chunks * rows * vocab,
    )


def _turn_kernel(chunks, perm, *refs):
    out = refs[-1]
    pairs, fars, fs = refs[:8], refs[8 : 8 + chunks], refs[8 + chunks : 8 + 2 * chunks]
    half, width = pairs[0].shape
    rows = half // 2
    feats = width - LANES
    for k in range(4):
        for h in range(2):
            out[_place(perm[k], LANES), h * half : (h + 1) * half] = jnp.transpose(pairs[2 * k + h][:, feats:])
    for k, parts in ((4, fars), (6, fs)):
        for side in range(2):
            whole = jnp.concatenate([x[side * rows : (side + 1) * rows, feats:] for x in parts], axis=0)
            out[_place(perm[k + side], LANES), :] = jnp.transpose(whole)


def _turn(perm, pairs, fars, fs):
    rows_all = 2 * pairs[0].shape[0]
    return _kernel(
        functools.partial(_turn_kernel, len(fars)),
        [pltpu.VMEM((8 * LANES, rows_all), BF16)],
        [perm, *pairs, *fars, *fs],
        "turned_features",
        specs=[SMEM] + [VMEM] * (8 + 2 * len(fars)),
        flops=16 * LANES * rows_all,
    )[0]


def _gradient(features, which, grad, out, scale):
    part = out.shape[0] // 4
    half = features.shape[0] // 2
    for c in _columns(grad.shape[1], 256):
        product = _dot(features[_place(which, half), :], grad[:, c]) * scale
        for b in range(4):
            out[b * part : (b + 1) * part, c] = product[b * LANES : b * LANES + part].astype(out.dtype)


def _send_kernel(tokens, tok, features, slope, scaled, inner, grad, out):
    chunks, rows = inner.shape[0] // 2, inner.shape[1]
    eye = _eye(rows)
    for i in range(chunks):
        column = _to_column(eye, inner[2 * i + 1 : 2 * i + 2, :])
        for r in range(0, rows, BLOCK):
            here = slice(i * rows + r, i * rows + r + BLOCK)
            grad[here, :] = (scaled[here, :] * (slope[here, :] - column[r : r + BLOCK])).astype(BF16)
    _gradient(features, 1 - tok[0], grad, out, 1.0 / tokens)


def _send(tok, features, slope, scaled, inner, tokens, part):
    rows_all, vocab = slope.shape
    return _kernel(
        functools.partial(_send_kernel, tokens),
        [pltpu.VMEM((rows_all, vocab), BF16), pltpu.VMEM((part, vocab), BF16)],
        [tok, features, slope, scaled, inner],
        "gradient_to_send",
        specs=[SMEM] + [VMEM] * 4,
        flops=features.shape[0] * rows_all * vocab,
    )


def _keep_kernel(tokens, tok, features, grad, out):
    _gradient(features, tok[0], grad, out, 1.0 / tokens)


def _keep(tok, features, grad, tokens, part):
    rows_all, vocab = grad.shape
    return _kernel(
        functools.partial(_keep_kernel, tokens),
        [pltpu.VMEM((part, vocab), F32)],
        [tok, features, grad],
        "gradient_to_keep",
        specs=[SMEM, VMEM, VMEM],
        flops=features.shape[0] * rows_all * vocab,
    )[0]


def _add_kernel(keep, received, out):
    out[...] = (keep[...] + received[...].astype(F32)).astype(out.dtype)


def _add(keep, received):
    return _kernel(
        _add_kernel,
        [jax.ShapeDtypeStruct(keep.shape, BF16)],
        [keep, received],
        "summed_gradient",
        out_specs=[pl.BlockSpec()],
        flops=keep.size,
    )[0]


class _Slots:
    def __init__(self):
        self.before, self.last, self.now = [], [], []

    def next(self):
        self.before, self.last, self.now = self.last, self.now, []

    def move(self, x, pairs, *after):
        if self.before or after:
            x = lax.optimization_barrier((x, *self.before, *after))[0]
        y = lax.ppermute(x, "voc", pairs)
        self.now.append(y)
        return y


def _xor(k):
    return [(i, i ^ k) for i in range(8)]


MIDDLE = [(2, 4), (4, 2), (3, 5), (5, 3)]
OUTWARD = [(2, 0), (3, 1), (4, 6), (5, 7)]


def _all_reduce(x, merge):
    for k in (1, 2, 4):
        x = merge(x, lax.ppermute(x, "voc", _xor(k)))
    return x


def _merge_softmax(a, b):
    top = jnp.maximum(a[0], b[0])
    return jnp.stack([top, a[1] * jnp.exp(a[0] - top) + b[1] * jnp.exp(b[0] - top)])


def _body_4x2(target_hidden, draft_hidden, target_head, draft_head):
    rows_all = target_hidden.shape[0]
    part, vocab = draft_head.shape
    chunks = 4
    rows = rows_all // chunks
    full = float(vocab * lax.axis_size("voc"))
    tokens = float(rows_all * lax.axis_size("tok"))
    me, tok = lax.axis_index("voc"), lax.axis_index("tok")
    z, x = me // 2, me % 2
    end = (z == 0) | (z == 3)
    far_z = (jnp.where(z < 2, 2, 1), jnp.where(z < 2, 3, 0))
    perm = [me, me ^ 2, me ^ 1, me ^ 3] + [2 * fz + side for side in (x, 1 - x) for fz in far_z]
    perm = jnp.stack(perm).astype(jnp.int32)
    tok_index = tok.reshape(1).astype(jnp.int32)

    halves = _pack(target_hidden, draft_hidden)
    wt = _fetch(target_head)
    wd = _head(tok_index, draft_head, lax.ppermute(draft_head, "tok", [(0, 1), (1, 0)]))

    slots = _Slots()
    p1, o, a, middle, outward, far, f, acc, es_t, es_d = ([] for _ in range(10))
    stats = jnp.zeros((2, 2 * chunks, rows), F32)
    done = []

    def near_pair(c):
        start = (c % 2) * rows
        return jnp.concatenate([h[start : start + rows] for h in (halves[c // 2], p1[c // 2])])

    for slot in range(8):
        if slot < 2:
            p1.append(slots.move(halves[slot], _xor(2)))
            o.append(slots.move(halves[slot], _xor(1)))
        elif slot < 4:
            a.append(slots.move(p1[slot - 2], _xor(1)))
        if 2 <= slot < 6:
            outward.append(slots.move(middle[slot - 2], OUTWARD, *done))
        if 1 <= slot < 5:
            middle.append(slots.move(near_pair(slot - 1), MIDDLE, *done))
        if slot >= 4:
            c = slot - 4
            far.append(jnp.where(end, outward[c], middle[c]))
            f.append(slots.move(far[c], _xor(1), *done))
        done = []
        if slot in (4, 5):
            h = slot - 4
            acc.append(_near(perm, halves[h], p1[h], o[h], a[h], wt, wd))
            done = [acc[h][0]]
        if slot >= 6:
            e_t, e_d, stats = _far(slot - 6, perm, far[slot - 6], f[slot - 6], wt, wd, acc[0], stats)
            es_t.append(e_t)
            es_d.append(e_d)
            done = [e_t]
        slots.next()
    for c in (2, 3):
        e_t, e_d, stats = _far(c, perm, far[c], f[c], wt, wd, acc[1], stats)
        es_t.append(e_t)
        es_d.append(e_d)

    total = _all_reduce(stats, _merge_softmax)
    slope, scaled, sums = _slopes(es_t, es_d, stats, total, full)
    pairs = [m[h] for m in (halves, p1, o, a) for h in range(2)]
    features = _turn(perm, pairs, far, f)
    sums = _all_reduce(sums, jnp.add)
    grad, send = _send(tok_index, features, slope, scaled, sums, tokens, part)
    received = lax.ppermute(send, "tok", [(0, 1), (1, 0)])
    keep = _keep(tok_index, features, grad, tokens, part)
    row_loss = sums.reshape(chunks, 2, rows)[:, 0].reshape(rows_all)
    return row_loss, _add(keep, received)


def _body_any(target_hidden, draft_hidden, target_head, draft_head):
    rows, vocab = target_hidden.shape[0], target_head.shape[1]
    full = float(vocab * lax.axis_size("voc"))
    tokens = float(rows * lax.axis_size("tok"))
    draft_weights = lax.all_gather(draft_head, "tok", axis=0, tiled=True)
    hidden = lax.all_gather(target_hidden, "voc", axis=1, tiled=True)
    target_logits = jnp.dot(hidden, target_head, preferred_element_type=F32)
    features = lax.all_gather(draft_hidden, "voc", axis=1, tiled=True)
    draft_logits = jnp.dot(features, draft_weights, preferred_element_type=F32)
    top_t, top_d = lax.pmax((jnp.max(target_logits, axis=1), jnp.max(draft_logits, axis=1)), "voc")
    target_exp = jnp.exp(target_logits - top_t[:, None])
    draft_exp = jnp.exp(draft_logits - top_d[:, None])
    total_t, total_d = lax.psum((jnp.sum(target_exp, axis=1), jnp.sum(draft_exp, axis=1)), "voc")
    target_prob = target_exp / total_t[:, None]
    draft_prob = draft_exp / total_d[:, None]
    spread = full * (draft_prob - target_prob)
    root = jnp.sqrt(spread * spread + 1.0)
    slope = spread / root
    loss = jnp.sum(root - 1.0, axis=1) / (2.0 * full)
    row_loss, inner = lax.psum((loss, jnp.sum(draft_prob * slope, axis=1)), "voc")
    logit_grad = (full * draft_prob * (slope - inner[:, None])).astype(BF16)
    summed = lax.dot_general(features, logit_grad, (((0,), (0,)), ((), ())), preferred_element_type=F32)
    draft_grad = lax.psum_scatter((summed / tokens).astype(BF16), "tok", scatter_dimension=0, tiled=True)
    return row_loss, draft_grad


def solution(mesh):
    body = _body_4x2 if (mesh.shape["voc"], mesh.shape["tok"]) == (8, 2) else _body_any
    return jax.shard_map(
        body,
        mesh=mesh,
        in_specs=(
            P(("grp", "tok"), "voc"),
            P(("grp", "tok"), "voc"),
            P(None, "voc"),
            P("tok", "voc"),
        ),
        out_specs=(P(("grp", "tok")), P(("grp", "tok"), "voc")),
        check_vma=False,
    )
```

```python
import functools

import jax
import jax.numpy as jnp
from jax import lax
from jax.experimental import pallas as pl
from jax.experimental.pallas import tpu as pltpu
from jax.sharding import PartitionSpec as P

F32, BF16 = jnp.float32, jnp.bfloat16
SCOPED_BYTES = 12 * 2**20
LANES = 128
BLOCK = 16

VMEM = pl.BlockSpec(memory_space=pltpu.VMEM)
SMEM = pl.BlockSpec(memory_space=pltpu.SMEM)
ANYWHERE = pl.BlockSpec(memory_space=pl.ANY)


def _kernel(body, outs, ins, name, flops=0, scratch=(), specs=None, out_specs=None, exps=0):
    specs = specs or [VMEM] * len(ins)
    ins = [pltpu.with_memory_space_constraint(x, pltpu.VMEM) if s is VMEM else x for x, s in zip(ins, specs, strict=True)]
    return pl.pallas_call(
        body,
        in_specs=specs,
        out_specs=out_specs or [VMEM] * len(outs),
        out_shape=outs,
        scratch_shapes=scratch,
        compiler_params=pltpu.CompilerParams(vmem_limit_bytes=SCOPED_BYTES),
        cost_estimate=pl.CostEstimate(
            flops=flops,
            bytes_accessed=sum(x.size * x.dtype.itemsize for x in ins),
            transcendentals=exps,
        ),
        name=name,
    )(*ins)


def _eye(n):
    return lax.broadcasted_iota(jnp.int32, (n, n), 0) == lax.broadcasted_iota(jnp.int32, (n, n), 1)


def _to_row(eye, column):
    return jnp.sum(jnp.where(eye, column, 0.0), axis=0, keepdims=True)


def _to_column(eye, row):
    return jnp.sum(jnp.where(eye, row, 0.0), axis=1, keepdims=True)


def _dot(a, b):
    return jnp.dot(a, b, preferred_element_type=F32)


def _place(index, size):
    return pl.ds(pl.multiple_of(index * size, size), size)


def _pack_kernel(starts, target, draft, *refs):
    *outs, drafts, sems = refs
    feats, draft_feats = target.shape[1], draft.shape[0]
    first = pltpu.make_async_copy(draft, drafts.at[:draft_feats, :], sems.at[len(outs)])
    first.start()
    copies = []
    for n, (out, start) in enumerate(zip(outs, starts, strict=True)):
        copies.append(
            pltpu.make_async_copy(target.at[start : start + out.shape[0], :], out.at[:, :feats], sems.at[n])
        )
        copies[-1].start()
    drafts[draft_feats:, :] = jnp.zeros((LANES - draft_feats, drafts.shape[1]), BF16)
    first.wait()
    turned = jnp.transpose(drafts[...])
    for out, start in zip(outs, starts, strict=True):
        out[:, feats:] = turned[start : start + out.shape[0], :]
    for copy in copies:
        copy.wait()


def _pack(target, draft, sizes, joint):
    rows_all, feats = target.shape
    starts = [sum(sizes[:n]) for n in range(len(sizes))]
    if joint:
        sizes, starts = [*sizes, sizes[0] + sizes[1]], [*starts, 0]
    hbm = pl.BlockSpec(memory_space=pltpu.HBM)
    return _kernel(
        functools.partial(_pack_kernel, starts),
        [pltpu.VMEM((rows, feats + LANES), BF16) for rows in sizes],
        [pltpu.with_memory_space_constraint(x, pltpu.HBM) for x in (target, draft.T)],
        "packed_hidden",
        specs=[hbm, hbm],
        scratch=[pltpu.VMEM((LANES, rows_all), BF16), pltpu.SemaphoreType.DMA((len(sizes) + 1,))],
    )


def _head_kernel(tok, mine, other, out):
    part = mine.shape[0] // 4
    out[...] = jnp.zeros_like(out)
    for which, ref in ((tok[0], mine), (1 - tok[0], other)):
        for b in range(4):
            start = pl.multiple_of(which * (4 * LANES) + b * LANES, LANES)
            out[pl.ds(start, part), :] = ref[b * part : (b + 1) * part, :]


def _head(tok, mine, other):
    plain = pl.BlockSpec()
    return _kernel(
        _head_kernel,
        [pltpu.VMEM((8 * LANES, mine.shape[1]), BF16)],
        [tok, mine, other],
        "draft_head",
        specs=[SMEM, plain, VMEM],
    )[0]


def _join_kernel(start, first, second, out):
    rows = out.shape[0] // 2
    out[:rows, :] = first[start : start + rows, :]
    out[rows:, :] = second[start : start + rows, :]


def _join(first, second, start, rows):
    out = pltpu.VMEM((2 * rows, first.shape[1]), first.dtype)
    return _kernel(functools.partial(_join_kernel, start), [out], [first, second], "joined_rows")[0]


def _columns(vocab, cols=256):
    return [slice(n, n + cols) for n in range(0, vocab, cols)]


def _accumulate(blocks, pieces, wt, wd, before, out_t, out_d, rows):
    feats = pieces[0][0].shape[1] - LANES
    xs = [ref[start : start + rows, :] for ref, start, _ in pieces]
    drafts = jnp.concatenate([x[:, feats:] for x in xs], axis=1)
    for c in _columns(wt.shape[1]):
        target = before[0][before[2] : before[2] + rows, c] if before else None
        for x, (_, _, block) in zip(xs, pieces, strict=True):
            term = _dot(x[:, :feats], wt[_place(blocks[block], feats), c])
            target = term if target is None else target + term
        head = jnp.concatenate([wd[_place(blocks[block], LANES), c] for _, _, block in pieces], axis=0)
        draft = _dot(drafts, head)
        out_t[:rows, c] = target
        out_d[:rows, c] = draft + before[1][before[2] : before[2] + rows, c] if before else draft


def _logits_kernel(where, start, rows, blocks, *refs):
    arrays, (wt, wd, *acc, out_t, out_d) = refs[: len(where)], refs[len(where) :]
    pieces = [(ref, first, block) for ref, group in zip(arrays, where, strict=True) for first, block in group]
    _accumulate(blocks, pieces, wt, wd, (*acc, start) if acc else None, out_t, out_d, rows)


def _logits(blocks, pieces, rows, wt, wd, acc=(), start=0):
    out = pltpu.VMEM((rows, wt.shape[1]), F32)
    where = [group for _, group in pieces]
    return _kernel(
        functools.partial(_logits_kernel, where, start, rows),
        [out, out],
        [blocks, *[array for array, _ in pieces], wt, wd, *acc],
        "logits",
        flops=2 * rows * pieces[0][0].shape[1] * wt.shape[1] * sum(map(len, where)),
        specs=[SMEM] + [VMEM] * (len(pieces) + 2 + len(acc)),
    )


def _exp_kernel(where, start, rows, index, extra, blocks, *refs):
    arrays, (wt, wd, acc_t, acc_d, *rest) = refs[: len(where)], refs[len(where) :]
    *more, before, e_t, e_d, stats = rest
    pieces = [(ref, first, block) for ref, group in zip(arrays, where, strict=True) for first, block in group]
    _accumulate(blocks, pieces, wt, wd, (acc_t, acc_d, start), e_t, e_d, rows)
    whole = rows + extra
    eye = _eye(whole)
    stats[...] = before[...]
    for kind, ref in enumerate((e_t, e_d)):
        tops, sums = [], []
        for r in range(0, whole, BLOCK):
            logits = ref[r : r + BLOCK, :] if r < rows else more[kind][r - rows : r - rows + BLOCK, :]
            top = jnp.max(logits, axis=1, keepdims=True)
            e = jnp.exp(logits - top)
            ref[r : r + BLOCK, :] = e
            tops.append(top)
            sums.append(jnp.sum(e, axis=1, keepdims=True))
        row = 2 * index + kind
        stats[0, row : row + 1, :whole] = _to_row(eye, jnp.concatenate(tops, axis=0))
        stats[1, row : row + 1, :whole] = _to_row(eye, jnp.concatenate(sums, axis=0))


def _exps(blocks, pieces, rows, wt, wd, acc, start, stats, index, more=()):
    extra = more[0].shape[0] if more else 0
    out = pltpu.VMEM((rows + extra, wt.shape[1]), F32)
    where = [group for _, group in pieces]
    return _kernel(
        functools.partial(_exp_kernel, where, start, rows, index, extra),
        [out, out, pltpu.VMEM(stats.shape, F32)],
        [blocks, *[array for array, _ in pieces], wt, wd, *acc, *more, stats],
        "exp_logits",
        flops=2 * rows * pieces[0][0].shape[1] * wt.shape[1] * sum(map(len, where)),
        exps=2 * (rows + extra) * wt.shape[1],
        specs=[SMEM] + [VMEM] * (len(pieces) + 5 + len(more)),
    )


def _slope_kernel(full, *refs):
    sets = (len(refs) - 5) // 2
    es_t, es_d = refs[:sets], refs[sets : 2 * sets]
    mine, total, slope_out, scaled_out, sums = refs[2 * sets :]
    sums[...] = jnp.zeros_like(sums)
    first = 0
    for i in range(sets):
        rows = es_t[i].shape[0]
        eye = _eye(rows)
        scales = [
            full
            * _to_column(
                eye,
                jnp.exp(mine[0, r : r + 1, :rows] - total[0, r : r + 1, :rows]) / total[1, r : r + 1, :rows],
            )
            for r in (2 * i, 2 * i + 1)
        ]
        losses, inners = [], []
        for r in range(0, rows, BLOCK):
            target = es_t[i][r : r + BLOCK, :] * scales[0][r : r + BLOCK]
            draft = es_d[i][r : r + BLOCK, :] * scales[1][r : r + BLOCK]
            spread = draft - target
            square = spread * spread + 1.0
            inverse = lax.rsqrt(square)
            slope = spread * inverse
            slope_out[first + r : first + r + BLOCK, :] = slope
            scaled_out[first + r : first + r + BLOCK, :] = draft
            losses.append(jnp.sum(square * inverse - 1.0, axis=1, keepdims=True))
            inners.append(jnp.sum(draft * slope, axis=1, keepdims=True))
        sums[2 * i : 2 * i + 1, :rows] = _to_row(eye, jnp.concatenate(losses, axis=0)) * (0.5 / full)
        sums[2 * i + 1 : 2 * i + 2, :rows] = _to_row(eye, jnp.concatenate(inners, axis=0)) * (1.0 / full)
        first += rows


def _slopes(es_t, es_d, mine, total, full):
    rows_all, vocab = sum(e.shape[0] for e in es_t), es_t[0].shape[1]
    out = pltpu.VMEM((rows_all, vocab), F32)
    return _kernel(
        functools.partial(_slope_kernel, full),
        [out, out, pltpu.VMEM(mine.shape[1:], F32)],
        [*es_t, *es_d, mine, total],
        "slopes",
        flops=12 * rows_all * vocab,
        exps=rows_all * vocab,
    )


def _turn_kernel(plan, blocks, *refs):
    out = refs[-1]
    feats = refs[0].shape[1] - LANES
    part = lambda ref, start, rows: refs[ref][start : start + rows, feats:]
    for block, rows_of in plan:
        columns = []
        for choices in rows_of:
            value = part(*choices[0])
            if len(choices) == 2:
                value = jnp.where(blocks[16] == 1, value, part(*choices[1]))
            columns.append(value)
        out[_place(blocks[block], LANES), :] = jnp.transpose(jnp.concatenate(columns, axis=0))


def _turn(blocks, arrays, plan, rows_all):
    return _kernel(
        functools.partial(_turn_kernel, plan),
        [pltpu.VMEM((8 * LANES, rows_all), BF16)],
        [blocks, *arrays],
        "turned_features",
        specs=[SMEM] + [VMEM] * len(arrays),
        flops=16 * LANES * rows_all,
    )[0]


def _gradient(features, which, grad, out, scale):
    part = out.shape[0] // 4
    half = features.shape[0] // 2
    for c in _columns(grad.shape[1], 256):
        product = _dot(features[_place(which, half), :], grad[:, c]) * scale
        for b in range(4):
            out[b * part : (b + 1) * part, c] = product[b * LANES : b * LANES + part].astype(out.dtype)


def _send_kernel(tokens, sizes, tok, features, slope, scaled, inner, grad, out):
    first = 0
    for i, rows in enumerate(sizes):
        column = _to_column(_eye(rows), inner[2 * i + 1 : 2 * i + 2, :rows])
        for r in range(0, rows, BLOCK):
            here = slice(first + r, first + r + BLOCK)
            grad[here, :] = (scaled[here, :] * (slope[here, :] - column[r : r + BLOCK])).astype(BF16)
        first += rows
    _gradient(features, 1 - tok[0], grad, out, 1.0 / tokens)


def _send(tok, features, slope, scaled, inner, tokens, sizes, part):
    rows_all, vocab = slope.shape
    return _kernel(
        functools.partial(_send_kernel, tokens, sizes),
        [pltpu.VMEM((rows_all, vocab), BF16), pltpu.VMEM((part, vocab), BF16)],
        [tok, features, slope, scaled, inner],
        "gradient_to_send",
        specs=[SMEM] + [VMEM] * 4,
        flops=features.shape[0] * rows_all * vocab,
    )


def _keep_kernel(tokens, tok, features, grad, out):
    _gradient(features, tok[0], grad, out, 1.0 / tokens)


def _keep(tok, features, grad, tokens, part):
    rows_all, vocab = grad.shape
    return _kernel(
        functools.partial(_keep_kernel, tokens),
        [pltpu.VMEM((part, vocab), F32)],
        [tok, features, grad],
        "gradient_to_keep",
        specs=[SMEM, VMEM, VMEM],
        flops=features.shape[0] * rows_all * vocab,
    )[0]


def _add_kernel(keep, received, out, came, summed, came_sem, out_sem):
    blocks, part = came.shape[:2]
    place = lambda b: slice(b * part, (b + 1) * part)
    fetch = [pltpu.make_async_copy(received.at[place(b), :], came.at[b], came_sem.at[b]) for b in range(blocks)]
    store = [pltpu.make_async_copy(summed.at[b], out.at[place(b), :], out_sem.at[b]) for b in range(blocks)]
    for copy in fetch:
        copy.start()
    for b in range(blocks):
        fetch[b].wait()
        summed[b] = (keep[place(b), :] + came[b].astype(F32)).astype(BF16)
        store[b].start()
    for copy in store:
        copy.wait()


def _add(keep, received):
    rows, vocab = keep.shape
    blocks = pltpu.VMEM((4, rows // 4, vocab), BF16)
    return _kernel(
        _add_kernel,
        [jax.ShapeDtypeStruct(keep.shape, BF16)],
        [keep, received],
        "summed_gradient",
        specs=[VMEM, ANYWHERE],
        out_specs=[ANYWHERE],
        scratch=[blocks, blocks, pltpu.SemaphoreType.DMA((4,)), pltpu.SemaphoreType.DMA((4,))],
        flops=keep.size,
    )[0]


REST = 64
MERGED = False
SLOTS = (
    ("O0", "S", "P0", "P1", "T",),
    ("M0", "O1",),
    ("M1", "U0", "A0",),
    ("M2", "U1", "A1",),
    ("M3", "U2", "F0",),
    ("U3", "F1",),
    ("X", "Y", "F2",),
    ("W", "F3",),
)
FREE = ("T",)
EARLY = ()
WORK = ((), (), (), (), ("G", "N0",), ("N1",), ("E0",), ("E1", "H",), ("R", "E2", "D", "E3",))


def _xor(k):
    return [(i, i ^ k) for i in range(8)]


MIDDLE = [(2, 4), (4, 2), (3, 5), (5, 3)]
OUTWARD = [(2, 0), (3, 1), (4, 6), (5, 7)]
PAIRS = {"S": _xor(1), "O": _xor(1), "A": _xor(1), "F": _xor(1), "P": _xor(2), "X": _xor(2), "Y": _xor(4), "W": _xor(6)}
PAIRS["T"] = [(0, 1), (1, 0)]
PAIRS |= {"M": MIDDLE, "U": OUTWARD}


def _all_reduce(x, merge):
    for k in (1, 2, 4):
        x = merge(x, lax.ppermute(x, "voc", _xor(k)))
    return x


def _merge_softmax(a, b):
    top = jnp.maximum(a[0], b[0])
    return jnp.stack([top, a[1] * jnp.exp(a[0] - top) + b[1] * jnp.exp(b[0] - top)])


def _body_4x2(target_hidden, draft_hidden, target_head, draft_head):
    rows_all = target_hidden.shape[0]
    part, vocab = draft_head.shape
    rest, chunks = REST, 4
    q = (rows_all - rest) // chunks
    sizes = (q, q, q, q + rest)
    full = float(vocab * lax.axis_size("voc"))
    tokens = float(rows_all * lax.axis_size("tok"))
    me, tok = lax.axis_index("voc"), lax.axis_index("tok")
    z, x = me // 2, me % 2
    end = (z == 0) | (z == 3)
    far_z = (jnp.where(z < 2, 2, 1), jnp.where(z < 2, 3, 0))
    blocks = [me, me ^ 2, me ^ 1, me ^ 3] + [2 * fz + side for side in (x, 1 - x) for fz in far_z]
    blocks = jnp.stack(blocks + [me ^ k for k in range(8)] + [end]).astype(jnp.int32)
    tok_index = tok.reshape(1).astype(jnp.int32)

    own0, own1, own_rest, *own_both = _pack(target_hidden, draft_hidden, [2 * q, 2 * q, rest], MERGED)
    own = (own0, own1)
    wt = target_head
    got, far, acc, wd = {}, {}, {}, None

    def rest_of(name):
        if name == "S" and "SS" not in got:
            got["SS"] = jnp.concatenate([own_rest, got["S"]])
        return got["SS" if name == "S" else name]

    def operand(name):
        kind, index = name[0], int(name[1:] or 0)
        if kind == "S":
            return own_rest
        if kind == "T":
            return draft_head
        if kind == "O" and MERGED:
            return own_both[0]
        if kind in "XYW":
            return rest_of("S")
        if kind in "PO":
            return own[index]
        if kind == "A":
            return got[f"P{index}"]
        if kind == "M":
            return jnp.concatenate([h[(index % 2) * q : (index % 2) * q + q] for h in (own[index // 2], got[f"P{index // 2}"])])
        if kind == "U":
            return got[f"M{index}"]
        far[index] = jnp.where(end, got[f"U{index}"], got[f"M{index}"])
        return far[index]

    def after(earlier):
        return lax.optimization_barrier((blocks, earlier))[0] if earlier is not None else blocks

    def other_x(h):
        return (got["O"], 2 * q * h) if MERGED else (got[f"O{h}"], 0)

    es_t, es_d, stats = [], [], jnp.zeros((2, 8, -(-max(sizes) // LANES) * LANES), F32)
    result = None

    def far_pieces(c):
        return [(far[c], [(0, 4), (q, 5)]), (got[f"F{c}"], [(0, 6), (q, 7)])]

    def rest_pieces(names, first):
        return [(rest_of(name), [(0, first + 2 * k), (rest, first + 2 * k + 1)]) for k, name in enumerate(names)]

    def work(name):
        nonlocal stats, result, wd
        tied = lax.optimization_barrier((blocks, result))[0] if result is not None else blocks
        kind, c = name[0], int(name[1:] or 0)
        if kind == "G":
            wd = result = _head(tok_index, draft_head, got["T"])
        elif kind == "N":
            pieces = ((own[c], 0), (got[f"P{c}"], 0), other_x(c), (got[f"A{c}"], 0))
            acc[c] = _logits(tied, [(array, [(at, k)]) for k, (array, at) in enumerate(pieces)], 2 * q, wt, wd)
            result = acc[c][0]
        elif kind in "HRD":
            if kind == "H":
                acc[kind] = _logits(tied, far_pieces(3)[:1], q, wt, wd, acc[1], q)
            elif kind == "R":
                acc[kind] = _logits(tied, rest_pieces("SX", 8), rest, wt, wd)
            else:
                acc[kind] = _logits(tied, rest_pieces("YW", 12), rest, wt, wd, acc["R"])
            result = acc[kind][0]
        else:
            last = c == chunks - 1
            e_t, e_d, stats = _exps(
                tied,
                far_pieces(c)[last:],
                q,
                wt,
                wd,
                acc["H"] if last else acc[c // 2],
                0 if last else (c % 2) * q,
                stats,
                c,
                acc["D"] if last else (),
            )
            es_t.append(e_t)
            es_d.append(e_d)
            result = e_t

    before, last, done = [], [], []
    for number, slot in enumerate(SLOTS):
        operands = [operand(name) for name in slot]
        for name, array in zip(slot, operands, strict=True):
            if before or done:
                array = lax.optimization_barrier((array, *before, *done))[0]
            got[name] = lax.ppermute(array, "tok" if name == "T" else "voc", PAIRS[name[0]])
        before = last + [got[name] for name in slot if name in EARLY]
        last, done = [got[name] for name in slot if name not in FREE + EARLY], []
        for name in WORK[number]:
            work(name)
            done = [result]
    for name in WORK[len(SLOTS)]:
        work(name)

    total = _all_reduce(stats, _merge_softmax)
    slope, scaled, sums = _slopes(es_t, es_d, stats, total, full)

    both = rest_of("S")
    arrays, plan = [], []

    def at(array, start, rows):
        arrays.append(array)
        return (len(arrays) - 1, start, rows)

    for k, (name, tail) in enumerate(((None, (both, 0)), ("P", (got["X"], 0)), ("O", (both, rest)), ("A", (got["X"], rest)))):
        if name is None:
            groups = [(g, 0) for g in own]
        elif name == "O":
            groups = [other_x(h) for h in range(2)]
        else:
            groups = [(got[f"{name}{h}"], 0) for h in range(2)]
        plan.append((k, [[at(*g, 2 * q)] for g in groups] + [[at(*tail, rest)]]))
    for k, (fars, side) in enumerate(((far, 0), (far, 1), ({c: got[f"F{c}"] for c in range(4)}, 0), ({c: got[f"F{c}"] for c in range(4)}, 1))):
        choices = [(got["Y"], (k // 2) * rest), (got["W"], (k // 2) * rest)]
        tail = [at(array, start, rest) for array, start in (choices if side == 0 else choices[::-1])]
        plan.append((4 + k, [[at(fars[c], side * q, q)] for c in range(4)] + [tail]))
    features = _turn(blocks, arrays, plan, rows_all)

    sums = _all_reduce(sums, jnp.add)
    grad, send = _send(tok_index, features, slope, scaled, sums, tokens, sizes, part)
    received = lax.ppermute(send, "tok", [(0, 1), (1, 0)])
    keep = _keep(tok_index, features, grad, tokens, part)
    row_loss = jnp.concatenate([sums[2 * i, :rows] for i, rows in enumerate(sizes)])
    return row_loss, _add(keep, received)


def _body_any(target_hidden, draft_hidden, target_head, draft_head):
    rows, vocab = target_hidden.shape[0], target_head.shape[1]
    full = float(vocab * lax.axis_size("voc"))
    tokens = float(rows * lax.axis_size("tok"))
    draft_weights = lax.all_gather(draft_head, "tok", axis=0, tiled=True)
    hidden = lax.all_gather(target_hidden, "voc", axis=1, tiled=True)
    target_logits = jnp.dot(hidden, target_head, preferred_element_type=F32)
    features = lax.all_gather(draft_hidden, "voc", axis=1, tiled=True)
    draft_logits = jnp.dot(features, draft_weights, preferred_element_type=F32)
    top_t, top_d = lax.pmax((jnp.max(target_logits, axis=1), jnp.max(draft_logits, axis=1)), "voc")
    target_exp = jnp.exp(target_logits - top_t[:, None])
    draft_exp = jnp.exp(draft_logits - top_d[:, None])
    total_t, total_d = lax.psum((jnp.sum(target_exp, axis=1), jnp.sum(draft_exp, axis=1)), "voc")
    target_prob = target_exp / total_t[:, None]
    draft_prob = draft_exp / total_d[:, None]
    spread = full * (draft_prob - target_prob)
    root = jnp.sqrt(spread * spread + 1.0)
    slope = spread / root
    loss = jnp.sum(root - 1.0, axis=1) / (2.0 * full)
    row_loss, inner = lax.psum((loss, jnp.sum(draft_prob * slope, axis=1)), "voc")
    logit_grad = (full * draft_prob * (slope - inner[:, None])).astype(BF16)
    summed = lax.dot_general(features, logit_grad, (((0,), (0,)), ((), ())), preferred_element_type=F32)
    draft_grad = lax.psum_scatter((summed / tokens).astype(BF16), "tok", scatter_dimension=0, tiled=True)
    return row_loss, draft_grad


def solution(mesh):
    body = _body_4x2 if (mesh.shape["voc"], mesh.shape["tok"]) == (8, 2) else _body_any
    return jax.shard_map(
        body,
        mesh=mesh,
        in_specs=(
            P(("grp", "tok"), "voc"),
            P(("grp", "tok"), "voc"),
            P(None, "voc"),
            P("tok", "voc"),
        ),
        out_specs=(P(("grp", "tok")), P(("grp", "tok"), "voc")),
        check_vma=False,
    )
```

```python
import functools

import jax
import jax.numpy as jnp
from jax import lax
from jax.experimental import pallas as pl
from jax.experimental.pallas import tpu as pltpu
from jax.sharding import PartitionSpec as P

F32, BF16 = jnp.float32, jnp.bfloat16
SCOPED_BYTES = 12 * 2**20
LANES = 128
BLOCK = 16

VMEM = pl.BlockSpec(memory_space=pltpu.VMEM)
SMEM = pl.BlockSpec(memory_space=pltpu.SMEM)
ANYWHERE = pl.BlockSpec(memory_space=pl.ANY)


def _kernel(body, outs, ins, name, flops=0, scratch=(), specs=None, out_specs=None, exps=0):
    specs = specs or [VMEM] * len(ins)
    ins = [pltpu.with_memory_space_constraint(x, pltpu.VMEM) if s is VMEM else x for x, s in zip(ins, specs, strict=True)]
    return pl.pallas_call(
        body,
        in_specs=specs,
        out_specs=out_specs or [VMEM] * len(outs),
        out_shape=outs,
        scratch_shapes=scratch,
        compiler_params=pltpu.CompilerParams(vmem_limit_bytes=SCOPED_BYTES),
        cost_estimate=pl.CostEstimate(
            flops=flops,
            bytes_accessed=sum(x.size * x.dtype.itemsize for x in ins),
            transcendentals=exps,
        ),
        name=name,
    )(*ins)


def _eye(n):
    return lax.broadcasted_iota(jnp.int32, (n, n), 0) == lax.broadcasted_iota(jnp.int32, (n, n), 1)


def _to_row(eye, column):
    return jnp.sum(jnp.where(eye, column, 0.0), axis=0, keepdims=True)


def _to_column(eye, row):
    return jnp.sum(jnp.where(eye, row, 0.0), axis=1, keepdims=True)


def _dot(a, b):
    return jnp.dot(a, b, preferred_element_type=F32)


def _place(index, size):
    return pl.ds(pl.multiple_of(index * size, size), size)


def _pack_kernel(starts, target, draft, *refs):
    *outs, drafts, sems = refs
    feats, draft_feats = target.shape[1], draft.shape[0]
    first = pltpu.make_async_copy(draft, drafts.at[:draft_feats, :], sems.at[len(outs)])
    first.start()
    copies = []
    for n, (out, start) in enumerate(zip(outs, starts, strict=True)):
        copies.append(
            pltpu.make_async_copy(target.at[start : start + out.shape[0], :], out.at[:, :feats], sems.at[n])
        )
        copies[-1].start()
    drafts[draft_feats:, :] = jnp.zeros((LANES - draft_feats, drafts.shape[1]), BF16)
    first.wait()
    turned = jnp.transpose(drafts[...])
    for out, start in zip(outs, starts, strict=True):
        out[:, feats:] = turned[start : start + out.shape[0], :]
    for copy in copies:
        copy.wait()


def _pack(target, draft, sizes, joint):
    rows_all, feats = target.shape
    starts = [sum(sizes[:n]) for n in range(len(sizes))]
    if joint:
        sizes, starts = [*sizes, sizes[0] + sizes[1]], [*starts, 0]
    hbm = pl.BlockSpec(memory_space=pltpu.HBM)
    return _kernel(
        functools.partial(_pack_kernel, starts),
        [pltpu.VMEM((rows, feats + LANES), BF16) for rows in sizes],
        [pltpu.with_memory_space_constraint(x, pltpu.HBM) for x in (target, draft.T)],
        "packed_hidden",
        specs=[hbm, hbm],
        scratch=[pltpu.VMEM((LANES, rows_all), BF16), pltpu.SemaphoreType.DMA((len(sizes) + 1,))],
    )


def _head_kernel(tok, mine, other, out):
    part = mine.shape[0] // 4
    out[...] = jnp.zeros_like(out)
    for which, ref in ((tok[0], mine), (1 - tok[0], other)):
        for b in range(4):
            start = pl.multiple_of(which * (4 * LANES) + b * LANES, LANES)
            out[pl.ds(start, part), :] = ref[b * part : (b + 1) * part, :]


def _head(tok, mine, other):
    plain = pl.BlockSpec()
    return _kernel(
        _head_kernel,
        [pltpu.VMEM((8 * LANES, mine.shape[1]), BF16)],
        [tok, mine, other],
        "draft_head",
        specs=[SMEM, plain, VMEM],
    )[0]


def _join_kernel(start, first, second, out):
    rows = out.shape[0] // 2
    out[:rows, :] = first[start : start + rows, :]
    out[rows:, :] = second[start : start + rows, :]


def _join(first, second, start, rows):
    out = pltpu.VMEM((2 * rows, first.shape[1]), first.dtype)
    return _kernel(functools.partial(_join_kernel, start), [out], [first, second], "joined_rows")[0]


def _columns(vocab, cols=256):
    return [slice(n, n + cols) for n in range(0, vocab, cols)]


def _accumulate(blocks, pieces, wt, wd, before, out_t, out_d, rows):
    feats = pieces[0][0].shape[1] - LANES
    xs = [ref[start : start + rows, :] for ref, start, _ in pieces]
    drafts = jnp.concatenate([x[:, feats:] for x in xs], axis=1)
    for c in _columns(wt.shape[1]):
        target = before[0][before[2] : before[2] + rows, c] if before else None
        for x, (_, _, block) in zip(xs, pieces, strict=True):
            term = _dot(x[:, :feats], wt[_place(blocks[block], feats), c])
            target = term if target is None else target + term
        head = jnp.concatenate([wd[_place(blocks[block], LANES), c] for _, _, block in pieces], axis=0)
        draft = _dot(drafts, head)
        out_t[:rows, c] = target
        out_d[:rows, c] = draft + before[1][before[2] : before[2] + rows, c] if before else draft


def _logits_kernel(where, start, rows, blocks, *refs):
    arrays, (wt, wd, *acc, out_t, out_d) = refs[: len(where)], refs[len(where) :]
    pieces = [(ref, first, block) for ref, group in zip(arrays, where, strict=True) for first, block in group]
    _accumulate(blocks, pieces, wt, wd, (*acc, start) if acc else None, out_t, out_d, rows)


def _logits(blocks, pieces, rows, wt, wd, acc=(), start=0):
    out = pltpu.VMEM((rows, wt.shape[1]), F32)
    where = [group for _, group in pieces]
    return _kernel(
        functools.partial(_logits_kernel, where, start, rows),
        [out, out],
        [blocks, *[array for array, _ in pieces], wt, wd, *acc],
        "logits",
        flops=2 * rows * pieces[0][0].shape[1] * wt.shape[1] * sum(map(len, where)),
        specs=[SMEM] + [VMEM] * (len(pieces) + 2 + len(acc)),
    )


def _exp_kernel(where, start, rows, index, extra, blocks, *refs):
    arrays, (wt, wd, acc_t, acc_d, *rest) = refs[: len(where)], refs[len(where) :]
    *more, before, e_t, e_d, stats = rest
    pieces = [(ref, first, block) for ref, group in zip(arrays, where, strict=True) for first, block in group]
    _accumulate(blocks, pieces, wt, wd, (acc_t, acc_d, start), e_t, e_d, rows)
    whole = rows + extra
    eye = _eye(whole)
    stats[...] = before[...]
    for kind, ref in enumerate((e_t, e_d)):
        tops, sums = [], []
        for r in range(0, whole, BLOCK):
            logits = ref[r : r + BLOCK, :] if r < rows else more[kind][r - rows : r - rows + BLOCK, :]
            top = jnp.max(logits, axis=1, keepdims=True)
            e = jnp.exp(logits - top)
            ref[r : r + BLOCK, :] = e
            tops.append(top)
            sums.append(jnp.sum(e, axis=1, keepdims=True))
        row = 2 * index + kind
        stats[0, row : row + 1, :whole] = _to_row(eye, jnp.concatenate(tops, axis=0))
        stats[1, row : row + 1, :whole] = _to_row(eye, jnp.concatenate(sums, axis=0))


def _exps(blocks, pieces, rows, wt, wd, acc, start, stats, index, more=()):
    extra = more[0].shape[0] if more else 0
    out = pltpu.VMEM((rows + extra, wt.shape[1]), F32)
    where = [group for _, group in pieces]
    return _kernel(
        functools.partial(_exp_kernel, where, start, rows, index, extra),
        [out, out, pltpu.VMEM(stats.shape, F32)],
        [blocks, *[array for array, _ in pieces], wt, wd, *acc, *more, stats],
        "exp_logits",
        flops=2 * rows * pieces[0][0].shape[1] * wt.shape[1] * sum(map(len, where)),
        exps=2 * (rows + extra) * wt.shape[1],
        specs=[SMEM] + [VMEM] * (len(pieces) + 5 + len(more)),
    )


def _slope_kernel(full, *refs):
    sets = (len(refs) - 5) // 2
    es_t, es_d = refs[:sets], refs[sets : 2 * sets]
    mine, total, slope_out, scaled_out, sums = refs[2 * sets :]
    sums[...] = jnp.zeros_like(sums)
    first = 0
    for i in range(sets):
        rows = es_t[i].shape[0]
        eye = _eye(rows)
        scales = [
            full
            * _to_column(
                eye,
                jnp.exp(mine[0, r : r + 1, :rows] - total[0, r : r + 1, :rows]) / total[1, r : r + 1, :rows],
            )
            for r in (2 * i, 2 * i + 1)
        ]
        losses, inners = [], []
        for r in range(0, rows, BLOCK):
            target = es_t[i][r : r + BLOCK, :] * scales[0][r : r + BLOCK]
            draft = es_d[i][r : r + BLOCK, :] * scales[1][r : r + BLOCK]
            spread = draft - target
            square = spread * spread + 1.0
            inverse = lax.rsqrt(square)
            slope = spread * inverse
            slope_out[first + r : first + r + BLOCK, :] = slope
            scaled_out[first + r : first + r + BLOCK, :] = draft
            losses.append(jnp.sum(square * inverse - 1.0, axis=1, keepdims=True))
            inners.append(jnp.sum(draft * slope, axis=1, keepdims=True))
        sums[2 * i : 2 * i + 1, :rows] = _to_row(eye, jnp.concatenate(losses, axis=0)) * (0.5 / full)
        sums[2 * i + 1 : 2 * i + 2, :rows] = _to_row(eye, jnp.concatenate(inners, axis=0)) * (1.0 / full)
        first += rows


def _slopes(es_t, es_d, mine, total, full):
    rows_all, vocab = sum(e.shape[0] for e in es_t), es_t[0].shape[1]
    out = pltpu.VMEM((rows_all, vocab), F32)
    return _kernel(
        functools.partial(_slope_kernel, full),
        [out, out, pltpu.VMEM(mine.shape[1:], F32)],
        [*es_t, *es_d, mine, total],
        "slopes",
        flops=12 * rows_all * vocab,
        exps=rows_all * vocab,
    )


def _turn_kernel(plan, blocks, *refs):
    out = refs[-1]
    feats = refs[0].shape[1] - LANES
    part = lambda ref, start, rows: refs[ref][start : start + rows, feats:]
    for block, rows_of in plan:
        columns = []
        for choices in rows_of:
            value = part(*choices[0])
            if len(choices) == 2:
                value = jnp.where(blocks[16] == 1, value, part(*choices[1]))
            columns.append(value)
        out[_place(blocks[block], LANES), :] = jnp.transpose(jnp.concatenate(columns, axis=0))


def _turn(blocks, arrays, plan, rows_all):
    return _kernel(
        functools.partial(_turn_kernel, plan),
        [pltpu.VMEM((8 * LANES, rows_all), BF16)],
        [blocks, *arrays],
        "turned_features",
        specs=[SMEM] + [VMEM] * len(arrays),
        flops=16 * LANES * rows_all,
    )[0]


def _gradient(features, which, grad, out, scale, first=0):
    part = out.shape[0] // 4
    half = features.shape[0] // 2
    for c in _columns(out.shape[1], 256):
        product = _dot(features[_place(which, half), :], grad[:, first + c.start : first + c.stop]) * scale
        for b in range(4):
            out[b * part : (b + 1) * part, c] = product[b * LANES : b * LANES + part].astype(out.dtype)


def _send_kernel(tokens, sizes, tok, features, slope, scaled, inner, grad, out):
    first = 0
    for i, rows in enumerate(sizes):
        column = _to_column(_eye(rows), inner[2 * i + 1 : 2 * i + 2, :rows])
        for r in range(0, rows, BLOCK):
            here = slice(first + r, first + r + BLOCK)
            grad[here, :] = (scaled[here, :] * (slope[here, :] - column[r : r + BLOCK])).astype(BF16)
        first += rows
    _gradient(features, 1 - tok[0], grad, out, 1.0 / tokens)


def _send(tok, features, slope, scaled, inner, tokens, sizes, part, cols):
    rows_all, vocab = slope.shape
    return _kernel(
        functools.partial(_send_kernel, tokens, sizes),
        [pltpu.VMEM((rows_all, vocab), BF16), pltpu.VMEM((part, cols), BF16)],
        [tok, features, slope, scaled, inner],
        "gradient_to_send",
        specs=[SMEM] + [VMEM] * 4,
        flops=features.shape[0] * rows_all * cols,
    )


def _more_kernel(tokens, first, tok, features, grad, out):
    _gradient(features, 1 - tok[0], grad, out, 1.0 / tokens, first)


def _more(tok, features, grad, tokens, part, first):
    rows_all, vocab = grad.shape
    return _kernel(
        functools.partial(_more_kernel, tokens, first),
        [pltpu.VMEM((part, vocab - first), BF16)],
        [tok, features, grad],
        "more_to_send",
        specs=[SMEM, VMEM, VMEM],
        flops=features.shape[0] * rows_all * (vocab - first),
    )[0]


def _keep_kernel(tokens, tok, features, grad, out):
    _gradient(features, tok[0], grad, out, 1.0 / tokens)


def _keep(tok, features, grad, tokens, part):
    rows_all, vocab = grad.shape
    return _kernel(
        functools.partial(_keep_kernel, tokens),
        [pltpu.VMEM((part, vocab), F32)],
        [tok, features, grad],
        "gradient_to_keep",
        specs=[SMEM, VMEM, VMEM],
        flops=features.shape[0] * rows_all * vocab,
    )[0]


def _add_kernel(keep, low, high, out, summed, sems):
    rows, first = low.shape
    part = rows // 4
    copies = []
    for b in range(4):
        here = slice(b * part, (b + 1) * part)
        summed[here, :first] = (keep[here, :first] + low[here, :].astype(F32)).astype(BF16)
        summed[here, first:] = (keep[here, first:] + high[here, :].astype(F32)).astype(BF16)
        copies.append(pltpu.make_async_copy(summed.at[here, :], out.at[here, :], sems.at[b]))
        copies[-1].start()
    for copy in copies:
        copy.wait()


def _add(keep, low, high):
    return _kernel(
        _add_kernel,
        [jax.ShapeDtypeStruct(keep.shape, BF16)],
        [keep, low, high],
        "summed_gradient",
        out_specs=[ANYWHERE],
        scratch=[pltpu.VMEM(keep.shape, BF16), pltpu.SemaphoreType.DMA((4,))],
        flops=keep.size,
    )[0]


REST = 64
MERGED = False
SLOTS = (
    ("O0", "S", "P0", "P1", "T",),
    ("M0", "O1",),
    ("M1", "U0", "A0",),
    ("M2", "U1", "A1",),
    ("M3", "U2", "F0",),
    ("U3", "F1",),
    ("X", "Y", "F2",),
    ("W", "F3",),
)
FREE = ("T",)
EARLY = ()
WORK = ((), (), (), (), ("G", "N0",), ("N1",), ("E0",), ("H", "E1",), ("R", "E2", "D", "E3",))


def _xor(k):
    return [(i, i ^ k) for i in range(8)]


MIDDLE = [(2, 4), (4, 2), (3, 5), (5, 3)]
OUTWARD = [(2, 0), (3, 1), (4, 6), (5, 7)]
PAIRS = {"S": _xor(1), "O": _xor(1), "A": _xor(1), "F": _xor(1), "P": _xor(2), "X": _xor(2), "Y": _xor(4), "W": _xor(6)}
PAIRS["T"] = [(0, 1), (1, 0)]
PAIRS |= {"M": MIDDLE, "U": OUTWARD}


def _all_reduce(x, merge):
    for k in (1, 2, 4):
        x = merge(x, lax.ppermute(x, "voc", _xor(k)))
    return x


def _merge_softmax(a, b):
    top = jnp.maximum(a[0], b[0])
    return jnp.stack([top, a[1] * jnp.exp(a[0] - top) + b[1] * jnp.exp(b[0] - top)])


def _body_4x2(target_hidden, draft_hidden, target_head, draft_head):
    rows_all = target_hidden.shape[0]
    part, vocab = draft_head.shape
    rest, chunks = REST, 4
    q = (rows_all - rest) // chunks
    sizes = (q, q, q, q + rest)
    full = float(vocab * lax.axis_size("voc"))
    tokens = float(rows_all * lax.axis_size("tok"))
    me, tok = lax.axis_index("voc"), lax.axis_index("tok")
    z, x = me // 2, me % 2
    end = (z == 0) | (z == 3)
    far_z = (jnp.where(z < 2, 2, 1), jnp.where(z < 2, 3, 0))
    blocks = [me, me ^ 2, me ^ 1, me ^ 3] + [2 * fz + side for side in (x, 1 - x) for fz in far_z]
    blocks = jnp.stack(blocks + [me ^ k for k in range(8)] + [end]).astype(jnp.int32)
    tok_index = tok.reshape(1).astype(jnp.int32)

    own0, own1, own_rest, *own_both = _pack(target_hidden, draft_hidden, [2 * q, 2 * q, rest], MERGED)
    own = (own0, own1)
    wt = target_head
    got, far, acc, wd = {}, {}, {}, None

    def rest_of(name):
        if name == "S" and "SS" not in got:
            got["SS"] = jnp.concatenate([own_rest, got["S"]])
        return got["SS" if name == "S" else name]

    def operand(name):
        kind, index = name[0], int(name[1:] or 0)
        if kind == "S":
            return own_rest
        if kind == "T":
            return draft_head
        if kind == "O" and MERGED:
            return own_both[0]
        if kind in "XYW":
            return rest_of("S")
        if kind in "PO":
            return own[index]
        if kind == "A":
            return got[f"P{index}"]
        if kind == "M":
            return jnp.concatenate([h[(index % 2) * q : (index % 2) * q + q] for h in (own[index // 2], got[f"P{index // 2}"])])
        if kind == "U":
            return got[f"M{index}"]
        far[index] = jnp.where(end, got[f"U{index}"], got[f"M{index}"])
        return far[index]

    def after(earlier):
        return lax.optimization_barrier((blocks, earlier))[0] if earlier is not None else blocks

    def other_x(h):
        return (got["O"], 2 * q * h) if MERGED else (got[f"O{h}"], 0)

    es_t, es_d, stats = [], [], jnp.zeros((2, 8, -(-max(sizes) // LANES) * LANES), F32)
    result = None

    def far_pieces(c):
        return [(far[c], [(0, 4), (q, 5)]), (got[f"F{c}"], [(0, 6), (q, 7)])]

    def rest_pieces(names, first):
        return [(rest_of(name), [(0, first + 2 * k), (rest, first + 2 * k + 1)]) for k, name in enumerate(names)]

    def work(name):
        nonlocal stats, result, wd
        tied = lax.optimization_barrier((blocks, result))[0] if result is not None else blocks
        kind, c = name[0], int(name[1:] or 0)
        if kind == "G":
            wd = result = _head(tok_index, draft_head, got["T"])
        elif kind == "N":
            pieces = ((own[c], 0), (got[f"P{c}"], 0), other_x(c), (got[f"A{c}"], 0))
            acc[c] = _logits(tied, [(array, [(at, k)]) for k, (array, at) in enumerate(pieces)], 2 * q, wt, wd)
            result = acc[c][0]
        elif kind in "HRD":
            if kind == "H":
                acc[kind] = _logits(tied, far_pieces(3)[:1], q, wt, wd, acc[1], q)
            elif kind == "R":
                acc[kind] = _logits(tied, rest_pieces("SX", 8), rest, wt, wd)
            else:
                acc[kind] = _logits(tied, rest_pieces("YW", 12), rest, wt, wd, acc["R"])
            result = acc[kind][0]
        else:
            last = c == chunks - 1
            e_t, e_d, stats = _exps(
                tied,
                far_pieces(c)[last:],
                q,
                wt,
                wd,
                acc["H"] if last else acc[c // 2],
                0 if last else (c % 2) * q,
                stats,
                c,
                acc["D"] if last else (),
            )
            es_t.append(e_t)
            es_d.append(e_d)
            result = e_t

    before, last, done = [], [], []
    for number, slot in enumerate(SLOTS):
        operands = [operand(name) for name in slot]
        for name, array in zip(slot, operands, strict=True):
            if before or done:
                array = lax.optimization_barrier((array, *before, *done))[0]
            got[name] = lax.ppermute(array, "tok" if name == "T" else "voc", PAIRS[name[0]])
        before = last + [got[name] for name in slot if name in EARLY]
        last, done = [got[name] for name in slot if name not in FREE + EARLY], []
        for name in WORK[number]:
            work(name)
            done = [result]
    for name in WORK[len(SLOTS)]:
        work(name)

    total = _all_reduce(stats, _merge_softmax)
    slope, scaled, sums = _slopes(es_t, es_d, stats, total, full)

    both = rest_of("S")
    arrays, plan = [], []

    def at(array, start, rows):
        arrays.append(array)
        return (len(arrays) - 1, start, rows)

    for k, (name, tail) in enumerate(((None, (both, 0)), ("P", (got["X"], 0)), ("O", (both, rest)), ("A", (got["X"], rest)))):
        if name is None:
            groups = [(g, 0) for g in own]
        elif name == "O":
            groups = [other_x(h) for h in range(2)]
        else:
            groups = [(got[f"{name}{h}"], 0) for h in range(2)]
        plan.append((k, [[at(*g, 2 * q)] for g in groups] + [[at(*tail, rest)]]))
    for k, (fars, side) in enumerate(((far, 0), (far, 1), ({c: got[f"F{c}"] for c in range(4)}, 0), ({c: got[f"F{c}"] for c in range(4)}, 1))):
        choices = [(got["Y"], (k // 2) * rest), (got["W"], (k // 2) * rest)]
        tail = [at(array, start, rest) for array, start in (choices if side == 0 else choices[::-1])]
        plan.append((4 + k, [[at(fars[c], side * q, q)] for c in range(4)] + [tail]))
    features = _turn(blocks, arrays, plan, rows_all)

    sums = _all_reduce(sums, jnp.add)
    cols = -(-vocab // 512) * 256
    grad, low = _send(tok_index, features, slope, scaled, sums, tokens, sizes, part, cols)
    low = lax.ppermute(low, "tok", PAIRS["T"])
    high = lax.ppermute(_more(tok_index, features, grad, tokens, part, cols), "tok", PAIRS["T"])
    keep = _keep(tok_index, features, grad, tokens, part)
    row_loss = jnp.concatenate([sums[2 * i, :rows] for i, rows in enumerate(sizes)])
    return row_loss, _add(keep, low, high)


def _body_any(target_hidden, draft_hidden, target_head, draft_head):
    rows, vocab = target_hidden.shape[0], target_head.shape[1]
    full = float(vocab * lax.axis_size("voc"))
    tokens = float(rows * lax.axis_size("tok"))
    draft_weights = lax.all_gather(draft_head, "tok", axis=0, tiled=True)
    hidden = lax.all_gather(target_hidden, "voc", axis=1, tiled=True)
    target_logits = jnp.dot(hidden, target_head, preferred_element_type=F32)
    features = lax.all_gather(draft_hidden, "voc", axis=1, tiled=True)
    draft_logits = jnp.dot(features, draft_weights, preferred_element_type=F32)
    top_t, top_d = lax.pmax((jnp.max(target_logits, axis=1), jnp.max(draft_logits, axis=1)), "voc")
    target_exp = jnp.exp(target_logits - top_t[:, None])
    draft_exp = jnp.exp(draft_logits - top_d[:, None])
    total_t, total_d = lax.psum((jnp.sum(target_exp, axis=1), jnp.sum(draft_exp, axis=1)), "voc")
    target_prob = target_exp / total_t[:, None]
    draft_prob = draft_exp / total_d[:, None]
    spread = full * (draft_prob - target_prob)
    root = jnp.sqrt(spread * spread + 1.0)
    slope = spread / root
    loss = jnp.sum(root - 1.0, axis=1) / (2.0 * full)
    row_loss, inner = lax.psum((loss, jnp.sum(draft_prob * slope, axis=1)), "voc")
    logit_grad = (full * draft_prob * (slope - inner[:, None])).astype(BF16)
    summed = lax.dot_general(features, logit_grad, (((0,), (0,)), ((), ())), preferred_element_type=F32)
    draft_grad = lax.psum_scatter((summed / tokens).astype(BF16), "tok", scatter_dimension=0, tiled=True)
    return row_loss, draft_grad


def solution(mesh):
    body = _body_4x2 if (mesh.shape["voc"], mesh.shape["tok"]) == (8, 2) else _body_any
    return jax.shard_map(
        body,
        mesh=mesh,
        in_specs=(
            P(("grp", "tok"), "voc"),
            P(("grp", "tok"), "voc"),
            P(None, "voc"),
            P("tok", "voc"),
        ),
        out_specs=(P(("grp", "tok")), P(("grp", "tok"), "voc")),
        check_vma=False,
    )
```
